512 devices in a mesh: patch: 64 (over x, y, z_lo), band: 8 (over z_hi, core).
Axes of the slice: x: 4, y: 4, z: 16 (z_hi: 4, z_lo: 4; z = z_hi * 4 + z_lo), core: 2. Of those that a mesh axis runs over, the one named last changes fastest.
Arguments:
- pixels: bfloat16 [16384, 16, 256], P('patch', 'band'), may hold values from -6 to 6
- cotangent: bfloat16 [16384, 1024], P('patch', 'band'), may hold values from -0.03125 to 0.03125
- avail: int32 [16, 16], P(None, 'band'), may hold values 0 or 1
- band_index: int32 [16], P('band'), may hold values from 0 to 207
- band_sensor: int32 [16], P('band'), may hold values from 0 to 3
- wave_table: float32 [208], replicated, may hold values from 0.4 to 12
- first_weight: float32 [128, 128], replicated, may hold values from -0.5 to 0.5
- sensor_embed: float32 [4, 128], replicated, may hold values from -6 to 6
- out_weight: bfloat16 [128, 1024, 256], P(None, 'patch'), may hold values from -0.0078125 to 0.0078125
Outputs:
- embed: bfloat16 [16384, 1024], P('patch', 'band')
- grad_out: float32 [128, 1024, 256], P(None, 'patch')
- grad_first: float32 [128, 128], replicated
- grad_sensor: float32 [4, 128], replicated
The draws below stay inside these ranges and needn't reach their ends.
All inputs are finite; a program needn't handle non-finite values. No bound on the sum of `avail` on one device may be relied on, other than what follows from the above.
Results may differ from the reference program's by a relative error of at most 0.017.
Values may be sent and summed in bfloat16 or wider, within the bound.
No kernel may reach another device: no remote copies, remote signals or barrier semaphores. Data moves between devices by JAX's collectives and lax.ppermute only.
A program may use at most 64 MiB of HBM per device.

```python
import math
import jax
import jax.numpy as jnp
from jax import lax

D = 1024
HID = 128
P2 = 256
WAVES = 208
SENSORS = 4
TILE_PATCHES = 1024
BAND_DEV = 2
PATCHES = 16384
BANDS = 16
TILES = 16
N_BAND = 8


def with_ends(result, own_key, least, top_value):
    place = [jax.random.randint(jax.random.fold_in(own_key, axis), (), 0, length) for axis, length in enumerate(result.shape)]
    main_axis = result.shape.index(max(result.shape))
    neighbour = place[:main_axis] + [(place[main_axis] + 1) % result.shape[main_axis]] + place[main_axis + 1:]
    return result.at[tuple(place)].set(least).at[tuple(neighbour)].set(top_value)


def raised(array, rng, source, target, blocks, factor):
    owner, partner = [(jnp.arange(array.shape[dim]) // (array.shape[dim] // blocks)).reshape([-1 if axis == dim else 1 for axis in range(array.ndim)]) for dim in (source, target)]
    chosen = jax.random.permutation(rng, blocks)[partner]
    strong = (owner == chosen) | (owner == (partner + blocks // 2) % blocks)
    return jnp.where(strong, factor * array, array)


def block_scale(own_key, dims, split, low, top_value):
    loudness = 1.0
    for axis_at, blocks in split:
        draws = jax.random.uniform(jax.random.fold_in(jax.random.fold_in(own_key, 6), axis_at), (blocks,), jnp.float32, low / len(split), top_value / len(split))
        loudness = loudness * jnp.repeat(jnp.exp(draws), dims[axis_at] // blocks).reshape((-1,) + (1,) * (len(dims) - 1 - axis_at))
    return loudness


def bell_draw(rng, shape, scale, most, cuts=(), held_as=jnp.bfloat16):
    entries = scale * jax.random.normal(rng, shape, jnp.float32)
    if cuts:
        entries = entries * block_scale(rng, shape, cuts, -0.22, 0.18)
    return jnp.clip(entries, -most, most).astype(held_as)


def bell_draw_with(rng, dims, scale, limit, cuts, heavy, kind=jnp.bfloat16):
    array = scale * jax.random.normal(rng, dims, jnp.float32)
    if cuts:
        array = array * block_scale(rng, dims, cuts, -0.22, 0.18)
    return jnp.clip(raised(array, jax.random.fold_in(rng, 3), *heavy), -limit, limit).astype(kind)


def setup_inputs(seed: int = 0) -> dict:
    splits = jax.random.split(jax.random.key(seed), 10)
    return {
        "pixels": bell_draw(splits[0], (PATCHES, BANDS, P2), 1.0, 6.0, ((0, 64), (1, 8))),
        "cotangent": bell_draw_with(splits[1], (PATCHES, D), (PATCHES * BANDS) ** -0.5, 0.03125, ((0, 64), (1, 8)), (0, 1, 64, 4.0)),
        "avail": with_ends((jax.random.randint(splits[2], (TILES, BANDS), 0, 4) < 3).astype(jnp.int32), jax.random.fold_in(splits[2], 1), 0, 1),
        "band_index": with_ends(jax.random.randint(splits[3], (BANDS,), 0, WAVES), jax.random.fold_in(splits[3], 1), 0, WAVES - 1).astype(jnp.int32),
        "band_sensor": with_ends(jax.random.randint(splits[4], (BANDS,), 0, SENSORS), jax.random.fold_in(splits[4], 1), 0, SENSORS - 1).astype(jnp.int32),
        "wave_table": jnp.clip(jnp.exp(jax.random.uniform(splits[5], (WAVES,), jnp.float32, math.log(0.4), math.log(12.0))), 0.4, 12.0),
        "first_weight": bell_draw(splits[6], (HID, HID), HID ** -0.5, 0.5, (), jnp.float32),
        "sensor_embed": bell_draw(splits[7], (SENSORS, HID), 1.0, 6.0, (), jnp.float32),
        "out_weight": bell_draw(splits[8], (HID, D, P2), (HID * BANDS * P2) ** -0.5, 0.0078125, ((1, 64),)),
    }


def wave_features(waves, width):
    half = width // 2
    steps = jnp.arange(half, dtype=jnp.float32)
    freqs = jnp.exp(steps * (math.log(100.0) / half))
    angles = waves[:, None] * freqs[None, :]
    return jnp.concatenate([jnp.sin(angles), jnp.cos(angles)], axis=1)


def silu_slope(preact):
    sigma = jax.nn.sigmoid(preact)
    return sigma * (1.0 + preact * (1.0 - sigma))


def reference(pixels, cotangent, avail, band_index, band_sensor, wave_table, first_weight, sensor_embed, out_weight):
    highest = lax.Precision.HIGHEST
    waves = wave_table[band_index]
    features = wave_features(waves, HID)
    sensor_hot = (band_sensor[:, None] == jnp.arange(SENSORS, dtype=jnp.int32)[None, :]).astype(jnp.float32)
    preact = jnp.dot(features, first_weight, precision=highest) + jnp.dot(sensor_hot, sensor_embed, precision=highest)
    hidden = jax.nn.silu(preact).astype(jnp.bfloat16)
    kernel = jnp.dot(hidden, out_weight.reshape(HID, D * P2), preferred_element_type=jnp.float32).astype(jnp.bfloat16)
    kernel = kernel.reshape(BANDS, D, P2)
    tile_of = jnp.arange(PATCHES, dtype=jnp.int32) // TILE_PATCHES
    row_mask = avail[tile_of].astype(jnp.bfloat16)
    masked = pixels * row_mask[:, :, None]
    flat_pixels = masked.reshape(PATCHES, BANDS * P2)
    flat_kernel = jnp.transpose(kernel, (0, 2, 1)).reshape(BANDS * P2, D)
    group_width = BAND_DEV * P2

    def add_group(group, total):
        offset = (group * jnp.int32(group_width)).astype(jnp.int32)
        left_part = lax.dynamic_slice_in_dim(flat_pixels, offset, group_width, 1)
        right_part = lax.dynamic_slice_in_dim(flat_kernel, offset, group_width, 0)
        partial_value = jnp.dot(left_part, right_part, preferred_element_type=jnp.float32)
        partial_value = lax.optimization_barrier(partial_value.astype(jnp.bfloat16)).astype(jnp.float32)
        return total + partial_value

    total = lax.fori_loop(jnp.int32(0), jnp.int32(N_BAND), add_group, jnp.zeros((PATCHES, D), jnp.float32))
    embed = total.astype(jnp.bfloat16)
    grad_kernel = jnp.dot(flat_pixels.T, cotangent, preferred_element_type=jnp.float32)
    grad_flat = jnp.transpose(grad_kernel.reshape(BANDS, P2, D), (0, 2, 1)).reshape(BANDS, D * P2)
    grad_out = jnp.dot(hidden.astype(jnp.float32).T, grad_flat, precision=highest).reshape(HID, D, P2)
    weight_flat = out_weight.astype(jnp.float32).reshape(HID, D * P2)
    grad_hidden = jnp.dot(grad_flat, weight_flat.T, precision=highest)
    grad_pre = grad_hidden * silu_slope(preact)
    grad_first = jnp.dot(features.T, grad_pre, precision=highest)
    grad_sensor = jnp.dot(sensor_hot.T, grad_pre, precision=highest)
    return embed, grad_out, grad_first, grad_sensor
```

```python
import functools
import math

import jax
import jax.numpy as jnp
from jax import lax
from jax.experimental import pallas as pl
from jax.experimental.pallas import tpu as pltpu
from jax.sharding import Mesh
from jax.sharding import PartitionSpec as P

TILE_PATCHES = 1024
X, Y, L, H, C = 4, 4, 4, 4, 2
BD = 2
DS = 16
P2 = 256
HID = 128
BF = jnp.bfloat16
F32 = jnp.float32
HIGHEST = lax.Precision.HIGHEST
VMEM = pl.BlockSpec(memory_space=pltpu.VMEM)
SMEM = pl.BlockSpec(memory_space=pltpu.SMEM)


def call(body, shape, dtype, specs, *args, flops=0, nbytes=2**20):
    return pl.pallas_call(
        body,
        out_shape=jax.ShapeDtypeStruct(shape, dtype),
        in_specs=specs,
        out_specs=VMEM,
        compiler_params=pltpu.CompilerParams(vmem_limit_bytes=24 * 2**20),
        cost_estimate=pl.CostEstimate(flops=flops, bytes_accessed=nbytes, transcendentals=0),
    )(*args)


def iota(shape, dim):
    return lax.broadcasted_iota(jnp.int32, shape, dim)


def wave_features(waves, width):
    half = width // 2
    steps = jnp.arange(half, dtype=F32)
    freqs = jnp.exp(steps * (math.log(100.0) / half))
    angles = waves[:, None] * freqs[None, :]
    return jnp.concatenate([jnp.sin(angles), jnp.cos(angles)], axis=1)


def silu_slope(preact):
    sigma = jax.nn.sigmoid(preact)
    return sigma * (1.0 + preact * (1.0 - sigma))


def hypernet(band_index, band_sensor, wave_table, first_weight, sensor_embed):
    table_hot = (
        band_index[:, None] == jnp.arange(wave_table.shape[0], dtype=jnp.int32)[None, :]
    ).astype(F32)
    waves = jnp.dot(table_hot, wave_table, precision=HIGHEST)
    features = wave_features(waves, first_weight.shape[0])
    sensor_hot = (
        band_sensor[:, None] == jnp.arange(sensor_embed.shape[0], dtype=jnp.int32)[None, :]
    ).astype(F32)
    preact = jnp.dot(features, first_weight, precision=HIGHEST) + jnp.dot(
        sensor_hot, sensor_embed, precision=HIGHEST
    )
    return (features, sensor_hot, preact)


def kernel_body(idx, sens, table, first, sensor, weight, out):
    lane = iota((8, HID), 1)
    half = HID // 2
    step = jnp.where(lane < half, lane, lane - half).astype(F32)
    freqs = jnp.exp(step * (math.log(100.0) / half))
    row = iota((8, HID), 0)
    waves = jnp.where(row == 0, table[idx[0]], table[idx[1]])
    angles = waves * freqs
    features = jnp.where(lane < half, jnp.sin(angles), jnp.cos(angles))
    preact = jnp.dot(features, first[...], precision=HIGHEST, preferred_element_type=F32)
    preact = preact + jnp.where(row == 0, sensor[pl.ds(sens[0], 1), :], sensor[pl.ds(sens[1], 1), :])
    hidden = (preact / (1.0 + jnp.exp(-preact))).astype(BF)
    wide = (iota((HID, HID * DS), 1) // DS == iota((HID, HID * DS), 0)).astype(F32).astype(BF)
    spread = jnp.dot(hidden, wide, preferred_element_type=F32)
    own = iota((DS, HID * DS), 1) % DS == iota((DS, HID * DS), 0)
    left = jnp.concatenate([jnp.where(own, spread[c : c + 1], 0.0) for c in range(BD)], axis=0).astype(BF)
    out[...] = jnp.dot(left, weight[...], preferred_element_type=F32).astype(BF)


def embed_body(masked, kernels, out):
    for b in range(H * C):
        total = None
        for c in range(BD):
            right = kernels[8 * b : 8 * b + 8, c].reshape(8 * DS, P2)
            term = lax.dot_general(
                masked[:, c * P2 : (c + 1) * P2], right, (((1,), (1,)), ((), ())), preferred_element_type=F32
            )
            total = term if total is None else total + term
        out[b] = total.astype(BF)


def grad_body(cot, masked, out):
    for b in range(H * C):
        block = cot[b % C, b // C, 0:256, :]
        part = lax.dot_general(block, masked[...], (((0,), (0,)), ((), ())), preferred_element_type=F32).astype(BF)
        for c in range(BD):
            out[8 * b : 8 * b + 8, c] = part[:, c * P2 : (c + 1) * P2].reshape(8, DS, P2)


def sum_xy_body(parts, out):
    total = parts[0].astype(F32)
    for i in range(1, X * Y):
        total = total + parts[i].astype(F32)
    total = total.astype(BF)
    for h in range(H):
        out[:, h] = total


def sum_l_body(parts, out):
    total = parts[0].astype(F32)
    for i in range(1, L):
        total = total + parts[i].astype(F32)
    out[...] = total.astype(BF)


def hidden_grad_body(grads, weight, out):
    rows = HID * DS
    n = H * C * BD * DS
    prod = lax.dot_general(weight[...], grads[...], (((1,), (1,)), ((), ())), preferred_element_type=F32)
    keep = iota((rows, n), 0) % DS == iota((rows, n), 1) % DS
    prod = jnp.where(keep, prod, 0.0).reshape(HID, DS, n).sum(axis=1)
    pick = (iota((n // DS, n), 1) // DS == iota((n // DS, n), 0)).astype(F32)
    out[...] = lax.dot_general(pick, prod, (((1,), (1,)), ((), ())), precision=HIGHEST, preferred_element_type=F32)


def out_grad_body(hidden_t, grads, out):
    n = H * C * BD * DS
    wide = (iota((n // DS, n), 1) // DS == iota((n // DS, n), 0)).astype(F32).astype(BF)
    spread = jnp.dot(hidden_t[...], wide, preferred_element_type=F32)
    keep = iota((DS, n), 0) == iota((DS, n), 1) % DS
    left = jnp.where(keep[None], spread[:, None, :], 0.0).reshape(HID * DS, n).astype(BF)
    out[...] = jnp.dot(left, grads[...], preferred_element_type=F32)


def gather(part, axes, count):
    return lax.all_to_all(jnp.broadcast_to(part[None], (count, *part.shape)), axes, 0, 0, tiled=True)


def local(
    pixels, cotangent, avail, band_index, band_sensor, wave_table, first_weight, sensor_embed, out_weight
):
    rows = pixels.shape[0]
    place = (lax.axis_index("x") * Y + lax.axis_index("y")) * L + lax.axis_index("l")
    tile = (place * rows) // TILE_PATCHES
    mask = lax.dynamic_slice_in_dim(avail, tile, 1, 0).astype(BF)
    masked = (pixels * mask[:, :, None]).reshape(rows, BD * P2)
    weight = out_weight.reshape(HID * DS, P2)

    ids = jnp.concatenate([band_index, band_sensor]).astype(BF)
    tail = jnp.pad(ids[None], ((0, 15), (0, cotangent.shape[1] - 2 * BD)))
    cot_h = gather(jnp.concatenate([cotangent, tail], axis=0), "h", H)
    cot = lax.all_gather(cot_h, "c", axis=0, tiled=False)

    part = call(
        kernel_body, (BD * DS, P2), BF, [SMEM, SMEM, SMEM, VMEM, VMEM, VMEM],
        band_index, band_sensor, wave_table, first_weight, sensor_embed, weight, flops=2**25,
    )
    part_l = gather(part, "l", L)
    kernels = gather(part_l.reshape(L * BD * DS, P2), ("x", "y"), X * Y).reshape(X * Y * L, BD, DS, P2)
    shares = call(embed_body, (H * C, rows, 128), BF, [VMEM, VMEM], masked, kernels, flops=2**28)
    embed = lax.psum_scatter(shares, ("h", "c"), scatter_dimension=0, tiled=False)

    grads = call(grad_body, (X * Y * L, BD, DS, P2), BF, [VMEM, VMEM], cot, masked, flops=2**28)
    grads = lax.all_to_all(grads.reshape(X * Y, L, BD * DS, P2), ("x", "y"), 0, 0, tiled=True)
    grads = call(sum_xy_body, (L, H, BD * DS, P2), BF, [VMEM], grads, flops=2**20)
    grads = lax.all_to_all(grads.reshape(L * H, BD * DS, P2), ("l", "h"), 0, 0, tiled=True)
    grads = call(sum_l_body, (H, BD * DS, P2), BF, [VMEM], grads.reshape(L, H, BD * DS, P2), flops=2**18)
    grads = lax.all_gather(grads, "c", axis=0, tiled=False).reshape(C * H * BD * DS, P2)

    every = cot[:, :, rows, : 2 * BD].astype(jnp.int32).reshape(C * H, 2 * BD)
    features, sensor_hot, preact = hypernet(
        every[:, :BD].reshape(-1), every[:, BD:].reshape(-1), wave_table, first_weight, sensor_embed
    )
    hidden_t = jax.nn.silu(preact).astype(BF).T
    slope = silu_slope(preact)

    part_hidden = call(hidden_grad_body, (C * H * BD, HID), F32, [VMEM, VMEM], grads, weight, flops=2**28)
    grad_hidden = gather(part_hidden, ("x", "y"), X * Y).sum(axis=0)
    grad_hidden = gather(grad_hidden, "l", L).sum(axis=0)
    grad_out = call(out_grad_body, (HID * DS, P2), F32, [VMEM, VMEM], hidden_t, grads, flops=2**28)
    grad_pre = grad_hidden * slope
    grad_first = jnp.dot(features.T, grad_pre, precision=HIGHEST)
    grad_sensor = jnp.dot(sensor_hot.T, grad_pre, precision=HIGHEST)
    return (embed, grad_out.reshape(HID, DS, P2), grad_first, grad_sensor)


def solution(mesh):
    fine = Mesh(mesh.devices.reshape(X, Y, L, H, C), ("x", "y", "l", "h", "c"))
    patch, band = ("x", "y", "l"), ("h", "c")
    return jax.shard_map(
        local,
        mesh=fine,
        in_specs=(
            P(patch, band, None),
            P(patch, band),
            P(None, band),
            P(band),
            P(band),
            P(),
            P(),
            P(),
            P(None, patch, None),
        ),
        out_specs=(P(patch, band), P(None, patch, None), P(), P()),
        check_vma=False,
    )
```

```python
import functools
import math

import jax
import jax.numpy as jnp
from jax import lax
from jax.experimental import pallas as pl
from jax.experimental.pallas import tpu as pltpu
from jax.sharding import Mesh
from jax.sharding import PartitionSpec as P

TILE_PATCHES = 1024
X, Y, L, H, C = 4, 4, 4, 4, 2
BD = 2
DS = 16
P2 = 256
HID = 128
BF = jnp.bfloat16
F32 = jnp.float32
HIGHEST = lax.Precision.HIGHEST
VMEM = pl.BlockSpec(memory_space=pltpu.VMEM)
SMEM = pl.BlockSpec(memory_space=pltpu.SMEM)


def call(body, outs, specs, *args, flops=0, nbytes=2**20, vmem=24):
    return pl.pallas_call(
        body,
        out_shape=[jax.ShapeDtypeStruct(shape, dtype) for shape, dtype in outs],
        in_specs=specs,
        out_specs=[VMEM] * len(outs),
        compiler_params=pltpu.CompilerParams(vmem_limit_bytes=vmem * 2**20),
        cost_estimate=pl.CostEstimate(flops=flops, bytes_accessed=nbytes, transcendentals=0),
    )(*args)


def iota(shape, dim):
    return lax.broadcasted_iota(jnp.int32, shape, dim)


def wave_features(waves, width):
    half = width // 2
    steps = jnp.arange(half, dtype=F32)
    freqs = jnp.exp(steps * (math.log(100.0) / half))
    angles = waves[:, None] * freqs[None, :]
    return jnp.concatenate([jnp.sin(angles), jnp.cos(angles)], axis=1)


def silu_slope(preact):
    sigma = jax.nn.sigmoid(preact)
    return sigma * (1.0 + preact * (1.0 - sigma))


def hypernet(band_index, band_sensor, wave_table, first_weight, sensor_embed):
    table_hot = (
        band_index[:, None] == jnp.arange(wave_table.shape[0], dtype=jnp.int32)[None, :]
    ).astype(F32)
    waves = jnp.dot(table_hot, wave_table, precision=HIGHEST)
    features = wave_features(waves, first_weight.shape[0])
    sensor_hot = (
        band_sensor[:, None] == jnp.arange(sensor_embed.shape[0], dtype=jnp.int32)[None, :]
    ).astype(F32)
    preact = jnp.dot(features, first_weight, precision=HIGHEST) + jnp.dot(
        sensor_hot, sensor_embed, precision=HIGHEST
    )
    return (features, sensor_hot, preact)


def kernel_body(idx, sens, table, first, sensor, weight, out):
    lane = iota((8, HID), 1)
    half = HID // 2
    step = jnp.where(lane < half, lane, lane - half).astype(F32)
    freqs = jnp.exp(step * (math.log(100.0) / half))
    row = iota((8, HID), 0)
    waves = jnp.where(row == 0, table[idx[0]], table[idx[1]])
    angles = waves * freqs
    features = jnp.where(lane < half, jnp.sin(angles), jnp.cos(angles))
    preact = jnp.dot(features, first[...], precision=HIGHEST, preferred_element_type=F32)
    preact = preact + jnp.where(row == 0, sensor[pl.ds(sens[0], 1), :], sensor[pl.ds(sens[1], 1), :])
    hidden = (preact / (1.0 + jnp.exp(-preact))).astype(BF)
    wide = (iota((HID, HID * DS), 1) // DS == iota((HID, HID * DS), 0)).astype(F32).astype(BF)
    spread = jnp.dot(hidden, wide, preferred_element_type=F32)
    own = iota((DS, HID * DS), 1) % DS == iota((DS, HID * DS), 0)
    left = jnp.concatenate([jnp.where(own, spread[c : c + 1], 0.0) for c in range(BD)], axis=0).astype(BF)
    part = jnp.dot(left, weight[...], preferred_element_type=F32).astype(BF)
    for to in range(L):
        out[to] = part


def embed_body(masked, kernels, keep, send):
    core, high = lax.axis_index("c"), lax.axis_index("h")
    for step in range(H):
        to = lax.rem(high + step, H)
        for out, side in ((keep, core), (send, 1 - core)):
            first = 8 * (to * C + side)
            total = None
            for c in range(BD):
                right = kernels[pl.ds(first, 8), c].reshape(8 * DS, P2)
                term = lax.dot_general(
                    masked[:, c * P2 : (c + 1) * P2], right, (((1,), (1,)), ((), ())), preferred_element_type=F32
                )
                total = term if total is None else total + term
            out[step] = total.astype(BF)


def pair_body(keep, other, *outs):
    for step in range(H):
        outs[step][...] = (keep[step].astype(F32) + other[step].astype(F32)).astype(BF)


def join_body(a, b, c, d, out):
    total = a[...].astype(F32) + b[...].astype(F32)
    out[...] = (total + c[...].astype(F32) + d[...].astype(F32)).astype(BF)


def grad_body(cot, masked, out):
    for b in range(H * C):
        block = cot[b % C, b // C, 0:256, :]
        part = lax.dot_general(block, masked[...], (((0,), (0,)), ((), ())), preferred_element_type=F32).astype(BF)
        for c in range(BD):
            out[8 * b : 8 * b + 8, c] = part[:, c * P2 : (c + 1) * P2].reshape(8, DS, P2)


def sum_xy_body(parts, out):
    total = parts[0].astype(F32)
    for i in range(1, X * Y):
        total = total + parts[i].astype(F32)
    total = total.astype(BF)
    for h in range(H):
        out[:, h] = total


def sum_l_body(parts, out):
    total = parts[0].astype(F32)
    for i in range(1, L):
        total = total + parts[i].astype(F32)
    out[...] = total.astype(BF)


def hidden_grad_body(grads, weight, out):
    rows = HID * DS
    n = H * BD * DS
    prod = lax.dot_general(weight[...], grads[...], (((1,), (1,)), ((), ())), preferred_element_type=F32)
    keep = iota((rows, n), 0) % DS == iota((rows, n), 1) % DS
    prod = jnp.where(keep, prod, 0.0).reshape(HID, DS, n).sum(axis=1)
    pick = (iota((n // DS, n), 1) // DS == iota((n // DS, n), 0)).astype(F32)
    part = lax.dot_general(pick, prod, (((1,), (1,)), ((), ())), precision=HIGHEST, preferred_element_type=F32)
    for to in range(X * Y):
        out[to] = part


def spread_body(parts, out):
    total = parts[0]
    for i in range(1, X * Y):
        total = total + parts[i]
    for to in range(L * C):
        out[to] = total


def final_body(parts, slope, features, sensor_hot, first, sensor):
    total = parts[0]
    for i in range(1, L):
        total = total + parts[i]
    grad_pre = total * slope[...]
    across = (((0,), (0,)), ((), ()))
    first[...] = lax.dot_general(features[...], grad_pre, across, precision=HIGHEST, preferred_element_type=F32)
    sensor[...] = lax.dot_general(sensor_hot[...], grad_pre, across, precision=HIGHEST, preferred_element_type=F32)


def out_grad_body(hidden_t, grads, out):
    n = H * C * BD * DS
    wide = (iota((n // DS, n), 1) // DS == iota((n // DS, n), 0)).astype(F32).astype(BF)
    spread = jnp.dot(hidden_t[...], wide, preferred_element_type=F32)
    keep = iota((DS, n), 0) == iota((DS, n), 1) % DS
    left = jnp.where(keep[None], spread[:, None, :], 0.0).reshape(HID * DS, n).astype(BF)
    out[...] = jnp.dot(left, grads[...], preferred_element_type=F32)


def gather(part, axes, count):
    return lax.all_to_all(jnp.broadcast_to(part[None], (count, *part.shape)), axes, 0, 0, tiled=True)


def local(
    pixels, cotangent, avail, band_index, band_sensor, wave_table, first_weight, sensor_embed, out_weight
):
    rows = pixels.shape[0]
    place = (lax.axis_index("x") * Y + lax.axis_index("y")) * L + lax.axis_index("l")
    tile = (place * rows) // TILE_PATCHES
    mask = lax.dynamic_slice_in_dim(avail, tile, 1, 0).astype(BF)
    masked = (pixels * mask[:, :, None]).reshape(rows, BD * P2)
    weight = out_weight.reshape(HID * DS, P2)

    (part,) = call(
        kernel_body, [((L, BD * DS, P2), BF)], [SMEM, SMEM, SMEM, VMEM, VMEM, VMEM],
        band_index, band_sensor, wave_table, first_weight, sensor_embed, weight, flops=2**25, vmem=60,
    )
    part_l = lax.all_to_all(part, "l", 0, 0, tiled=True)

    ids = jnp.concatenate([band_index, band_sensor]).astype(BF)
    tail = jnp.pad(ids[None], ((0, 15), (0, cotangent.shape[1] - 2 * BD)))
    cot_own = jnp.concatenate([cotangent, tail], axis=0)
    cot_own, part_l = lax.optimization_barrier((cot_own, part_l))
    kernels = gather(part_l.reshape(L * BD * DS, P2), ("x", "y"), X * Y).reshape(X * Y * L, BD, DS, P2)
    cot = lax.all_gather(lax.all_gather(cot_own, "h", axis=0, tiled=False), "c", axis=0, tiled=False)
    (grads,) = call(grad_body, [((X * Y * L, BD, DS, P2), BF)], [VMEM, VMEM], cot, masked, flops=2**28)

    grads, kernels = lax.optimization_barrier((grads, kernels))
    grads = lax.all_to_all(grads.reshape(X * Y, L, BD * DS, P2), ("x", "y"), 0, 0, tiled=True)
    shape = ((H, rows, 128), BF)
    keep, send = call(embed_body, [shape, shape], [VMEM, VMEM], masked, kernels, flops=2**28)
    other = lax.ppermute(send, "c", [(0, 1), (1, 0)])
    shares = call(pair_body, [((rows, 128), BF)] * H, [VMEM, VMEM], keep, other, flops=2**18)
    shares = [shares[0]] + [
        lax.ppermute(shares[step], "h", [(i, (i + step) % H) for i in range(H)]) for step in range(1, H)
    ]
    (embed,) = call(join_body, [((rows, 128), BF)], [VMEM] * H, *shares, flops=2**18)

    grads, *_ = lax.optimization_barrier((grads, shares[1]))
    (grads,) = call(sum_xy_body, [((L, H, BD * DS, P2), BF)], [VMEM], grads, flops=2**20)
    grads = lax.all_to_all(grads.reshape(L * H, BD * DS, P2), ("l", "h"), 0, 0, tiled=True)
    (grads,) = call(sum_l_body, [((H, BD * DS, P2), BF)], [VMEM], grads.reshape(L, H, BD * DS, P2), flops=2**18)
    mine = grads.reshape(H * BD * DS, P2)
    grads = lax.all_gather(mine, "c", axis=0, tiled=True)

    every = cot[:, :, rows, : 2 * BD].astype(jnp.int32).reshape(C * H, 2 * BD)
    features, sensor_hot, preact = hypernet(
        every[:, :BD].reshape(-1), every[:, BD:].reshape(-1), wave_table, first_weight, sensor_embed
    )
    hidden_t = jax.nn.silu(preact).astype(BF).T
    slope = silu_slope(preact)

    bands = C * H * BD
    (parts,) = call(hidden_grad_body, [((X * Y, bands // C, HID), F32)], [VMEM, VMEM], mine, weight, flops=2**28)
    parts = lax.all_to_all(parts, ("x", "y"), 0, 0, tiled=True)
    parts, *_ = lax.optimization_barrier((parts, shares[3]))
    (parts,) = call(spread_body, [((L * C, bands // C, HID), F32)], [VMEM], parts, flops=2**16)
    parts = lax.all_to_all(parts, ("l", "c"), 0, 0, tiled=True).reshape(L, bands, HID)
    (grad_out,) = call(out_grad_body, [((HID * DS, P2), F32)], [VMEM, VMEM], hidden_t, grads, flops=2**28)
    grad_first, grad_sensor = call(
        final_body, [(first_weight.shape, F32), (sensor_embed.shape, F32)], [VMEM] * 4,
        parts, slope, features, sensor_hot, flops=2**20,
    )
    return (embed, grad_out.reshape(HID, DS, P2), grad_first, grad_sensor)


def solution(mesh):
    fine = Mesh(mesh.devices.reshape(X, Y, L, H, C), ("x", "y", "l", "h", "c"))
    patch, band = ("x", "y", "l"), ("h", "c")
    return jax.shard_map(
        local,
        mesh=fine,
        in_specs=(
            P(patch, band, None),
            P(patch, band),
            P(None, band),
            P(band),
            P(band),
            P(),
            P(),
            P(),
            P(None, patch, None),
        ),
        out_specs=(P(patch, band), P(None, patch, None), P(), P()),
        check_vma=False,
    )
```

```python
import functools
import math

import jax
import jax.numpy as jnp
from jax import lax
from jax.experimental import pallas as pl
from jax.experimental.pallas import tpu as pltpu
from jax.sharding import Mesh
from jax.sharding import PartitionSpec as P

TILE_PATCHES = 1024
X, Y, L, H, C = 4, 4, 4, 4, 2
BD = 2
DS = 16
P2 = 256
HID = 128
BF = jnp.bfloat16
F32 = jnp.float32
HIGHEST = lax.Precision.HIGHEST
VMEM = pl.BlockSpec(memory_space=pltpu.VMEM)
SMEM = pl.BlockSpec(memory_space=pltpu.SMEM)


def call(body, outs, specs, *args, flops=0, nbytes=2**20, vmem=24):
    return pl.pallas_call(
        body,
        out_shape=[jax.ShapeDtypeStruct(shape, dtype) for shape, dtype in outs],
        in_specs=specs,
        out_specs=[VMEM] * len(outs),
        compiler_params=pltpu.CompilerParams(vmem_limit_bytes=vmem * 2**20),
        cost_estimate=pl.CostEstimate(flops=flops, bytes_accessed=nbytes, transcendentals=0),
    )(*args)


def iota(shape, dim):
    return lax.broadcasted_iota(jnp.int32, shape, dim)


def wave_features(waves, width):
    half = width // 2
    steps = jnp.arange(half, dtype=F32)
    freqs = jnp.exp(steps * (math.log(100.0) / half))
    angles = waves[:, None] * freqs[None, :]
    return jnp.concatenate([jnp.sin(angles), jnp.cos(angles)], axis=1)


def silu_slope(preact):
    sigma = jax.nn.sigmoid(preact)
    return sigma * (1.0 + preact * (1.0 - sigma))


def hypernet(band_index, band_sensor, wave_table, first_weight, sensor_embed):
    table_hot = (
        band_index[:, None] == jnp.arange(wave_table.shape[0], dtype=jnp.int32)[None, :]
    ).astype(F32)
    waves = jnp.dot(table_hot, wave_table, precision=HIGHEST)
    features = wave_features(waves, first_weight.shape[0])
    sensor_hot = (
        band_sensor[:, None] == jnp.arange(sensor_embed.shape[0], dtype=jnp.int32)[None, :]
    ).astype(F32)
    preact = jnp.dot(features, first_weight, precision=HIGHEST) + jnp.dot(
        sensor_hot, sensor_embed, precision=HIGHEST
    )
    return (features, sensor_hot, preact)


def kernel_body(idx, sens, table, first, sensor, weight, out):
    lane = iota((8, HID), 1)
    half = HID // 2
    step = jnp.where(lane < half, lane, lane - half).astype(F32)
    freqs = jnp.exp(step * (math.log(100.0) / half))
    row = iota((8, HID), 0)
    waves = jnp.where(row == 0, table[idx[0]], table[idx[1]])
    angles = waves * freqs
    features = jnp.where(lane < half, jnp.sin(angles), jnp.cos(angles))
    preact = jnp.dot(features, first[...], precision=HIGHEST, preferred_element_type=F32)
    preact = preact + jnp.where(row == 0, sensor[pl.ds(sens[0], 1), :], sensor[pl.ds(sens[1], 1), :])
    hidden = (preact / (1.0 + jnp.exp(-preact))).astype(BF)
    wide = (iota((HID, HID * DS), 1) // DS == iota((HID, HID * DS), 0)).astype(F32).astype(BF)
    spread = jnp.dot(hidden, wide, preferred_element_type=F32)
    own = iota((DS, HID * DS), 1) % DS == iota((DS, HID * DS), 0)
    left = jnp.concatenate([jnp.where(own, spread[c : c + 1], 0.0) for c in range(BD)], axis=0).astype(BF)
    part = jnp.dot(left, weight[...], preferred_element_type=F32).astype(BF)
    for to in range(L):
        out[to] = part


def embed_body(masked, kernels, keep, send):
    core, high = lax.axis_index("c"), lax.axis_index("h")
    for step in range(H):
        to = lax.rem(high + step, H)
        for out, side in ((keep, core), (send, 1 - core)):
            first = 8 * (to * C + side)
            total = None
            for c in range(BD):
                right = kernels[pl.ds(first, 8), c].reshape(8 * DS, P2)
                term = lax.dot_general(
                    masked[:, c * P2 : (c + 1) * P2], right, (((1,), (1,)), ((), ())), preferred_element_type=F32
                )
                total = term if total is None else total + term
            out[step] = total.astype(BF)


def pair_body(keep, other, *outs):
    for step in range(H):
        outs[step][...] = (keep[step].astype(F32) + other[step].astype(F32)).astype(BF)


def add_body(a, b, out):
    out[...] = (a[...].astype(F32) + b[...].astype(F32)).astype(BF)


def join_body(a, b, c, out):
    out[...] = (a[...].astype(F32) + b[...].astype(F32) + c[...].astype(F32)).astype(BF)


def grad_body(cot, masked, out):
    for b in range(H * C):
        block = cot[b % C, b // C, 0:256, :]
        part = lax.dot_general(block, masked[...], (((0,), (0,)), ((), ())), preferred_element_type=F32).astype(BF)
        for c in range(BD):
            out[8 * b : 8 * b + 8, c] = part[:, c * P2 : (c + 1) * P2].reshape(8, DS, P2)


def sum_xy_body(parts, out):
    total = parts[0].astype(F32)
    for i in range(1, X * Y):
        total = total + parts[i].astype(F32)
    total = total.astype(BF)
    for h in range(H):
        out[:, h] = total


def sum_l_body(parts, out):
    total = parts[0].astype(F32)
    for i in range(1, L):
        total = total + parts[i].astype(F32)
    out[...] = total.astype(BF)


def hidden_grad_body(grads, weight, out):
    rows = HID * DS
    n = H * BD * DS
    prod = lax.dot_general(weight[...], grads[...], (((1,), (1,)), ((), ())), preferred_element_type=F32)
    keep = iota((rows, n), 0) % DS == iota((rows, n), 1) % DS
    prod = jnp.where(keep, prod, 0.0).reshape(HID, DS, n).sum(axis=1)
    pick = (iota((n // DS, n), 1) // DS == iota((n // DS, n), 0)).astype(F32)
    part = lax.dot_general(pick, prod, (((1,), (1,)), ((), ())), precision=HIGHEST, preferred_element_type=F32)
    for to in range(X * Y):
        out[to] = part


def spread_body(parts, out):
    total = parts[0]
    for i in range(1, X * Y):
        total = total + parts[i]
    for to in range(L * C):
        out[to] = total


def final_body(parts, slope, features, sensor_hot, first, sensor):
    total = parts[0]
    for i in range(1, L):
        total = total + parts[i]
    grad_pre = total * slope[...]
    across = (((0,), (0,)), ((), ()))
    first[...] = lax.dot_general(features[...], grad_pre, across, precision=HIGHEST, preferred_element_type=F32)
    sensor[...] = lax.dot_general(sensor_hot[...], grad_pre, across, precision=HIGHEST, preferred_element_type=F32)


def out_grad_body(hidden_t, grads, out):
    n = H * C * BD * DS
    wide = (iota((n // DS, n), 1) // DS == iota((n // DS, n), 0)).astype(F32).astype(BF)
    spread = jnp.dot(hidden_t[...], wide, preferred_element_type=F32)
    keep = iota((DS, n), 0) == iota((DS, n), 1) % DS
    left = jnp.where(keep[None], spread[:, None, :], 0.0).reshape(HID * DS, n).astype(BF)
    out[...] = jnp.dot(left, grads[...], preferred_element_type=F32)


def gather(part, axes, count):
    return lax.all_to_all(jnp.broadcast_to(part[None], (count, *part.shape)), axes, 0, 0, tiled=True)


def local(
    pixels, cotangent, avail, band_index, band_sensor, wave_table, first_weight, sensor_embed, out_weight
):
    rows = pixels.shape[0]
    place = (lax.axis_index("x") * Y + lax.axis_index("y")) * L + lax.axis_index("l")
    tile = (place * rows) // TILE_PATCHES
    mask = lax.dynamic_slice_in_dim(avail, tile, 1, 0).astype(BF)
    masked = (pixels * mask[:, :, None]).reshape(rows, BD * P2)
    weight = out_weight.reshape(HID * DS, P2)

    (part,) = call(
        kernel_body, [((L, BD * DS, P2), BF)], [SMEM, SMEM, SMEM, VMEM, VMEM, VMEM],
        band_index, band_sensor, wave_table, first_weight, sensor_embed, weight, flops=2**25, vmem=60,
    )
    part_l = lax.all_to_all(part, "l", 0, 0, tiled=True)

    ids = jnp.concatenate([band_index, band_sensor]).astype(BF)
    tail = jnp.pad(ids[None], ((0, 15), (0, cotangent.shape[1] - 2 * BD)))
    cot_own = jnp.concatenate([cotangent, tail], axis=0)
    cot_own, part_l = lax.optimization_barrier((cot_own, part_l))
    kernels = gather(part_l.reshape(L * BD * DS, P2), ("x", "y"), X * Y).reshape(X * Y * L, BD, DS, P2)
    cot = lax.all_gather(lax.all_gather(cot_own, "h", axis=0, tiled=False), "c", axis=0, tiled=False)
    (grads,) = call(grad_body, [((X * Y * L, BD, DS, P2), BF)], [VMEM, VMEM], cot, masked, flops=2**28)

    grads, kernels = lax.optimization_barrier((grads, kernels))
    grads = lax.all_to_all(grads.reshape(X * Y, L, BD * DS, P2), ("x", "y"), 0, 0, tiled=True)
    shape = ((H, rows, 128), BF)
    keep, send = call(embed_body, [shape, shape], [VMEM, VMEM], masked, kernels, flops=2**28)
    other = lax.ppermute(send, "c", [(0, 1), (1, 0)])
    shares = call(pair_body, [((rows, 128), BF)] * H, [VMEM, VMEM], keep, other, flops=2**18)
    up, down = [(i, (i + 1) % H) for i in range(H)], [(i, (i - 1) % H) for i in range(H)]
    first = lax.ppermute(shares[2], "h", up)
    third = lax.ppermute(shares[3], "h", down)
    (second,) = call(add_body, [((rows, 128), BF)], [VMEM] * 2, shares[1], first, flops=2**16)
    second = lax.ppermute(second, "h", up)

    grads, *_ = lax.optimization_barrier((grads, first, third))
    (grads,) = call(sum_xy_body, [((L, H, BD * DS, P2), BF)], [VMEM], grads, flops=2**20)
    grads = lax.all_to_all(grads.reshape(L * H, BD * DS, P2), ("l", "h"), 0, 0, tiled=True)
    (grads,) = call(sum_l_body, [((H, BD * DS, P2), BF)], [VMEM], grads.reshape(L, H, BD * DS, P2), flops=2**18)
    mine = grads.reshape(H * BD * DS, P2)
    grads = lax.all_gather(mine, "c", axis=0, tiled=True)

    every = cot[:, :, rows, : 2 * BD].astype(jnp.int32).reshape(C * H, 2 * BD)
    features, sensor_hot, preact = hypernet(
        every[:, :BD].reshape(-1), every[:, BD:].reshape(-1), wave_table, first_weight, sensor_embed
    )
    hidden_t = jax.nn.silu(preact).astype(BF).T
    slope = silu_slope(preact)

    (embed,) = call(join_body, [((rows, 128), BF)], [VMEM] * 3, shares[0], second, third, flops=2**18)
    bands = C * H * BD
    (parts,) = call(hidden_grad_body, [((X * Y, bands // C, HID), F32)], [VMEM, VMEM], mine, weight, flops=2**28)
    parts = lax.all_to_all(parts, ("x", "y"), 0, 0, tiled=True)
    (grad_out,) = call(out_grad_body, [((HID * DS, P2), F32)], [VMEM, VMEM], hidden_t, grads, flops=2**28)
    parts, *_ = lax.optimization_barrier((parts, grad_out))
    parts, *_ = lax.optimization_barrier((parts, second))
    (parts,) = call(spread_body, [((L * C, bands // C, HID), F32)], [VMEM], parts, flops=2**16)
    parts = lax.all_to_all(parts, ("l", "c"), 0, 0, tiled=True).reshape(L, bands, HID)
    grad_first, grad_sensor = call(
        final_body, [(first_weight.shape, F32), (sensor_embed.shape, F32)], [VMEM] * 4,
        parts, slope, features, sensor_hot, flops=2**20,
    )
    return (embed, grad_out.reshape(HID, DS, P2), grad_first, grad_sensor)


def solution(mesh):
    fine = Mesh(mesh.devices.reshape(X, Y, L, H, C), ("x", "y", "l", "h", "c"))
    patch, band = ("x", "y", "l"), ("h", "c")
    return jax.shard_map(
        local,
        mesh=fine,
        in_specs=(
            P(patch, band, None),
            P(patch, band),
            P(None, band),
            P(band),
            P(band),
            P(),
            P(),
            P(),
            P(None, patch, None),
        ),
        out_specs=(P(patch, band), P(None, patch, None), P(), P()),
        check_vma=False,
    )
```

```python
import functools
import math

import jax
import jax.numpy as jnp
from jax import lax
from jax.experimental import pallas as pl
from jax.experimental.pallas import tpu as pltpu
from jax.sharding import Mesh
from jax.sharding import PartitionSpec as P

TILE_PATCHES = 1024
X, Y, L, H, C = 4, 4, 4, 4, 2
BD = 2
DS = 16
P2 = 256
HID = 128
BF = jnp.bfloat16
F32 = jnp.float32
HIGHEST = lax.Precision.HIGHEST
VMEM = pl.BlockSpec(memory_space=pltpu.VMEM)
SMEM = pl.BlockSpec(memory_space=pltpu.SMEM)


def call(body, outs, specs, *args, flops=0, nbytes=2**20, vmem=24):
    return pl.pallas_call(
        body,
        out_shape=[jax.ShapeDtypeStruct(shape, dtype) for shape, dtype in outs],
        in_specs=specs,
        out_specs=[VMEM] * len(outs),
        compiler_params=pltpu.CompilerParams(vmem_limit_bytes=vmem * 2**20),
        cost_estimate=pl.CostEstimate(flops=flops, bytes_accessed=nbytes, transcendentals=0),
    )(*args)


def iota(shape, dim):
    return lax.broadcasted_iota(jnp.int32, shape, dim)


def wave_features(waves, width):
    half = width // 2
    steps = jnp.arange(half, dtype=F32)
    freqs = jnp.exp(steps * (math.log(100.0) / half))
    angles = waves[:, None] * freqs[None, :]
    return jnp.concatenate([jnp.sin(angles), jnp.cos(angles)], axis=1)


def silu_slope(preact):
    sigma = jax.nn.sigmoid(preact)
    return sigma * (1.0 + preact * (1.0 - sigma))


def hypernet(band_index, band_sensor, wave_table, first_weight, sensor_embed):
    table_hot = (
        band_index[:, None] == jnp.arange(wave_table.shape[0], dtype=jnp.int32)[None, :]
    ).astype(F32)
    waves = jnp.dot(table_hot, wave_table, precision=HIGHEST)
    features = wave_features(waves, first_weight.shape[0])
    sensor_hot = (
        band_sensor[:, None] == jnp.arange(sensor_embed.shape[0], dtype=jnp.int32)[None, :]
    ).astype(F32)
    preact = jnp.dot(features, first_weight, precision=HIGHEST) + jnp.dot(
        sensor_hot, sensor_embed, precision=HIGHEST
    )
    return (features, sensor_hot, preact)


def kernel_body(idx, sens, table, first, sensor, weight, out):
    lane = iota((8, HID), 1)
    half = HID // 2
    step = jnp.where(lane < half, lane, lane - half).astype(F32)
    freqs = jnp.exp(step * (math.log(100.0) / half))
    row = iota((8, HID), 0)
    waves = jnp.where(row == 0, table[idx[0]], table[idx[1]])
    angles = waves * freqs
    features = jnp.where(lane < half, jnp.sin(angles), jnp.cos(angles))
    preact = jnp.dot(features, first[...], precision=HIGHEST, preferred_element_type=F32)
    preact = preact + jnp.where(row == 0, sensor[pl.ds(sens[0], 1), :], sensor[pl.ds(sens[1], 1), :])
    hidden = (preact / (1.0 + jnp.exp(-preact))).astype(BF)
    wide = (iota((HID, HID * DS), 1) // DS == iota((HID, HID * DS), 0)).astype(F32).astype(BF)
    spread = jnp.dot(hidden, wide, preferred_element_type=F32)
    own = iota((DS, HID * DS), 1) % DS == iota((DS, HID * DS), 0)
    left = jnp.concatenate([jnp.where(own, spread[c : c + 1], 0.0) for c in range(BD)], axis=0).astype(BF)
    part = jnp.dot(left, weight[...], preferred_element_type=F32).astype(BF)
    for to in range(L):
        out[to] = part


def embed_body(masked, kernels, keep, send):
    core, high = lax.axis_index("c"), lax.axis_index("h")
    for step in range(H):
        to = lax.rem(high + step, H)
        for out, side in ((keep, core), (send, 1 - core)):
            first = 8 * (to * C + side)
            total = None
            for c in range(BD):
                right = kernels[pl.ds(first, 8), c].reshape(8 * DS, P2)
                term = lax.dot_general(
                    masked[:, c * P2 : (c + 1) * P2], right, (((1,), (1,)), ((), ())), preferred_element_type=F32
                )
                total = term if total is None else total + term
            out[step] = total.astype(BF)


def pair_body(keep, other, *outs):
    for step in range(H):
        outs[step][...] = (keep[step].astype(F32) + other[step].astype(F32)).astype(BF)


def add_body(a, b, out):
    out[...] = (a[...].astype(F32) + b[...].astype(F32)).astype(BF)


def join_body(a, b, c, out):
    out[...] = (a[...].astype(F32) + b[...].astype(F32) + c[...].astype(F32)).astype(BF)


def grad_body(cot, masked, out):
    for b in range(H * C):
        block = cot[b // C, b % C, 0:256, :]
        part = lax.dot_general(block, masked[...], (((0,), (0,)), ((), ())), preferred_element_type=F32).astype(BF)
        for c in range(BD):
            out[8 * b : 8 * b + 8, c] = part[:, c * P2 : (c + 1) * P2].reshape(8, DS, P2)


def sum_xy_body(parts, out):
    total = parts[0].astype(F32)
    for i in range(1, X * Y):
        total = total + parts[i].astype(F32)
    total = total.astype(BF)
    for h in range(H):
        out[:, h] = total


def sum_l_body(parts, out):
    total = parts[0].astype(F32)
    for i in range(1, L):
        total = total + parts[i].astype(F32)
    out[...] = total.astype(BF)


def hidden_grad_body(grads, weight, out):
    rows = HID * DS
    n = H * BD * DS
    prod = lax.dot_general(weight[...], grads[...], (((1,), (1,)), ((), ())), preferred_element_type=F32)
    keep = iota((rows, n), 0) % DS == iota((rows, n), 1) % DS
    prod = jnp.where(keep, prod, 0.0).reshape(HID, DS, n).sum(axis=1)
    pick = (iota((n // DS, n), 1) // DS == iota((n // DS, n), 0)).astype(F32)
    part = lax.dot_general(pick, prod, (((1,), (1,)), ((), ())), precision=HIGHEST, preferred_element_type=F32)
    for to in range(X * Y):
        out[to] = part


def spread_body(parts, out):
    total = parts[0]
    for i in range(1, X * Y):
        total = total + parts[i]
    for to in range(L * C):
        out[to] = total


def final_body(parts, slope, features, sensor_hot, first, sensor):
    total = parts[0]
    for i in range(1, L):
        total = total + parts[i]
    grad_pre = total * slope[...]
    across = (((0,), (0,)), ((), ()))
    first[...] = lax.dot_general(features[...], grad_pre, across, precision=HIGHEST, preferred_element_type=F32)
    sensor[...] = lax.dot_general(sensor_hot[...], grad_pre, across, precision=HIGHEST, preferred_element_type=F32)


def out_grad_body(hidden_t, grads, out):
    n = H * C * BD * DS
    wide = (iota((n // DS, n), 1) // DS == iota((n // DS, n), 0)).astype(F32).astype(BF)
    spread = jnp.dot(hidden_t[...], wide, preferred_element_type=F32)
    keep = iota((DS, n), 0) == iota((DS, n), 1) % DS
    left = jnp.where(keep[None], spread[:, None, :], 0.0).reshape(HID * DS, n).astype(BF)
    out[...] = jnp.dot(left, grads[...], preferred_element_type=F32)


def gather(part, axes, count):
    return lax.all_to_all(jnp.broadcast_to(part[None], (count, *part.shape)), axes, 0, 0, tiled=True)


def local(
    pixels, cotangent, avail, band_index, band_sensor, wave_table, first_weight, sensor_embed, out_weight
):
    rows = pixels.shape[0]
    place = (lax.axis_index("x") * Y + lax.axis_index("y")) * L + lax.axis_index("l")
    tile = (place * rows) // TILE_PATCHES
    mask = lax.dynamic_slice_in_dim(avail, tile, 1, 0).astype(BF)
    masked = (pixels * mask[:, :, None]).reshape(rows, BD * P2)
    weight = out_weight.reshape(HID * DS, P2)

    (part,) = call(
        kernel_body, [((L, BD * DS, P2), BF)], [SMEM, SMEM, SMEM, VMEM, VMEM, VMEM],
        band_index, band_sensor, wave_table, first_weight, sensor_embed, weight, flops=2**25, vmem=60,
    )
    part_l = lax.all_to_all(part, "l", 0, 0, tiled=True)

    ids = jnp.concatenate([band_index, band_sensor]).astype(BF)
    tail = jnp.pad(ids[None], ((0, 15), (0, cotangent.shape[1] - 2 * BD)))
    cot_own = jnp.concatenate([cotangent, tail], axis=0)
    cot_own, part_l = lax.optimization_barrier((cot_own, part_l))
    kernels = gather(part_l.reshape(L * BD * DS, P2), ("x", "y"), X * Y).reshape(X * Y * L, BD, DS, P2)
    cot = lax.all_gather(cot_own, ("h", "c"), axis=0, tiled=False).reshape(H, C, rows + 16, 128)
    (grads,) = call(grad_body, [((X * Y * L, BD, DS, P2), BF)], [VMEM, VMEM], cot, masked, flops=2**28)

    grads, kernels = lax.optimization_barrier((grads, kernels))
    grads = lax.all_to_all(grads.reshape(X * Y, L, BD * DS, P2), ("x", "y"), 0, 0, tiled=True)
    shape = ((H, rows, 128), BF)
    keep, send = call(embed_body, [shape, shape], [VMEM, VMEM], masked, kernels, flops=2**28)
    other = lax.ppermute(send, "c", [(0, 1), (1, 0)])
    shares = call(pair_body, [((rows, 128), BF)] * H, [VMEM, VMEM], keep, other, flops=2**18)
    up, down = [(i, (i + 1) % H) for i in range(H)], [(i, (i - 1) % H) for i in range(H)]
    first = lax.ppermute(shares[2], "h", up)
    third = lax.ppermute(shares[3], "h", down)
    (second,) = call(add_body, [((rows, 128), BF)], [VMEM] * 2, shares[1], first, flops=2**16)
    second = lax.ppermute(second, "h", up)

    grads, *_ = lax.optimization_barrier((grads, first, third))
    (grads,) = call(sum_xy_body, [((L, H, BD * DS, P2), BF)], [VMEM], grads, flops=2**20)
    grads = lax.all_to_all(grads.reshape(L * H, BD * DS, P2), ("l", "h"), 0, 0, tiled=True)
    (grads,) = call(sum_l_body, [((H, BD * DS, P2), BF)], [VMEM], grads.reshape(L, H, BD * DS, P2), flops=2**18)
    mine = grads.reshape(H * BD * DS, P2)
    grads = lax.all_gather(mine, "c", axis=0, tiled=True)

    every = cot[:, :, rows, : 2 * BD].astype(jnp.int32).swapaxes(0, 1).reshape(C * H, 2 * BD)
    features, sensor_hot, preact = hypernet(
        every[:, :BD].reshape(-1), every[:, BD:].reshape(-1), wave_table, first_weight, sensor_embed
    )
    hidden_t = jax.nn.silu(preact).astype(BF).T
    slope = silu_slope(preact)

    (embed,) = call(join_body, [((rows, 128), BF)], [VMEM] * 3, shares[0], second, third, flops=2**18)
    bands = C * H * BD
    (parts,) = call(hidden_grad_body, [((X * Y, bands // C, HID), F32)], [VMEM, VMEM], mine, weight, flops=2**28)
    parts = lax.all_to_all(parts, ("x", "y"), 0, 0, tiled=True)
    (grad_out,) = call(out_grad_body, [((HID * DS, P2), F32)], [VMEM, VMEM], hidden_t, grads, flops=2**28)
    parts, *_ = lax.optimization_barrier((parts, grad_out))
    parts, *_ = lax.optimization_barrier((parts, second))
    (parts,) = call(spread_body, [((L * C, bands // C, HID), F32)], [VMEM], parts, flops=2**16)
    parts = lax.all_to_all(parts, ("l", "c"), 0, 0, tiled=True).reshape(L, bands, HID)
    grad_first, grad_sensor = call(
        final_body, [(first_weight.shape, F32), (sensor_embed.shape, F32)], [VMEM] * 4,
        parts, slope, features, sensor_hot, flops=2**20,
    )
    return (embed, grad_out.reshape(HID, DS, P2), grad_first, grad_sensor)


def solution(mesh):
    fine = Mesh(mesh.devices.reshape(X, Y, L, H, C), ("x", "y", "l", "h", "c"))
    patch, band = ("x", "y", "l"), ("h", "c")
    return jax.shard_map(
        local,
        mesh=fine,
        in_specs=(
            P(patch, band, None),
            P(patch, band),
            P(None, band),
            P(band),
            P(band),
            P(),
            P(),
            P(),
            P(None, patch, None),
        ),
        out_specs=(P(patch, band), P(None, patch, None), P(), P()),
        check_vma=False,
    )
```

```python
import functools
import math

import jax
import jax.numpy as jnp
from jax import lax
from jax.experimental import pallas as pl
from jax.experimental.pallas import tpu as pltpu
from jax.sharding import Mesh
from jax.sharding import PartitionSpec as P

TILE_PATCHES = 1024
X, Y, L, H, C = 4, 4, 4, 4, 2
BD = 2
DS = 16
P2 = 256
HID = 128
BF = jnp.bfloat16
F32 = jnp.float32
HIGHEST = lax.Precision.HIGHEST
VMEM = pl.BlockSpec(memory_space=pltpu.VMEM)
SMEM = pl.BlockSpec(memory_space=pltpu.SMEM)


def call(body, outs, specs, *args, flops=0, nbytes=2**20, vmem=24):
    return pl.pallas_call(
        body,
        out_shape=[jax.ShapeDtypeStruct(shape, dtype) for shape, dtype in outs],
        in_specs=specs,
        out_specs=[VMEM] * len(outs),
        compiler_params=pltpu.CompilerParams(vmem_limit_bytes=vmem * 2**20),
        cost_estimate=pl.CostEstimate(flops=flops, bytes_accessed=nbytes, transcendentals=0),
    )(*args)


def iota(shape, dim):
    return lax.broadcasted_iota(jnp.int32, shape, dim)


def wave_features(waves, width):
    half = width // 2
    steps = jnp.arange(half, dtype=F32)
    freqs = jnp.exp(steps * (math.log(100.0) / half))
    angles = waves[:, None] * freqs[None, :]
    return jnp.concatenate([jnp.sin(angles), jnp.cos(angles)], axis=1)


def silu_slope(preact):
    sigma = jax.nn.sigmoid(preact)
    return sigma * (1.0 + preact * (1.0 - sigma))


def hypernet(band_index, band_sensor, wave_table, first_weight, sensor_embed):
    table_hot = (
        band_index[:, None] == jnp.arange(wave_table.shape[0], dtype=jnp.int32)[None, :]
    ).astype(F32)
    waves = jnp.dot(table_hot, wave_table, precision=HIGHEST)
    features = wave_features(waves, first_weight.shape[0])
    sensor_hot = (
        band_sensor[:, None] == jnp.arange(sensor_embed.shape[0], dtype=jnp.int32)[None, :]
    ).astype(F32)
    preact = jnp.dot(features, first_weight, precision=HIGHEST) + jnp.dot(
        sensor_hot, sensor_embed, precision=HIGHEST
    )
    return (features, sensor_hot, preact)


def kernel_body(idx, sens, table, first, sensor, weight, out):
    lane = iota((8, HID), 1)
    half = HID // 2
    step = jnp.where(lane < half, lane, lane - half).astype(F32)
    freqs = jnp.exp(step * (math.log(100.0) / half))
    row = iota((8, HID), 0)
    waves = jnp.where(row == 0, table[idx[0]], table[idx[1]])
    angles = waves * freqs
    features = jnp.where(lane < half, jnp.sin(angles), jnp.cos(angles))
    preact = jnp.dot(features, first[...], precision=HIGHEST, preferred_element_type=F32)
    preact = preact + jnp.where(row == 0, sensor[pl.ds(sens[0], 1), :], sensor[pl.ds(sens[1], 1), :])
    hidden = (preact / (1.0 + jnp.exp(-preact))).astype(BF)
    wide = (iota((HID, HID * DS), 1) // DS == iota((HID, HID * DS), 0)).astype(F32).astype(BF)
    spread = jnp.dot(hidden, wide, preferred_element_type=F32)
    own = iota((DS, HID * DS), 1) % DS == iota((DS, HID * DS), 0)
    left = jnp.concatenate([jnp.where(own, spread[c : c + 1], 0.0) for c in range(BD)], axis=0).astype(BF)
    part = jnp.dot(left, weight[...], preferred_element_type=F32).astype(BF)
    for to in range(L):
        out[to] = part


def embed_body(masked, kernels, keep, send):
    core, high = lax.axis_index("c"), lax.axis_index("h")
    for step in range(H):
        to = lax.rem(high + step, H)
        for out, side in ((keep, core), (send, 1 - core)):
            first = 8 * (to * C + side)
            total = None
            for c in range(BD):
                right = kernels[pl.ds(first, 8), c].reshape(8 * DS, P2)
                term = lax.dot_general(
                    masked[:, c * P2 : (c + 1) * P2], right, (((1,), (1,)), ((), ())), preferred_element_type=F32
                )
                total = term if total is None else total + term
            out[step] = total.astype(BF)


def pair_body(keep, other, *outs):
    for step in range(H):
        outs[step][...] = (keep[step].astype(F32) + other[step].astype(F32)).astype(BF)


def add_body(a, b, out):
    out[...] = (a[...].astype(F32) + b[...].astype(F32)).astype(BF)


def join_body(a, b, c, out):
    out[...] = (a[...].astype(F32) + b[...].astype(F32) + c[...].astype(F32)).astype(BF)


def grad_body(cot, masked, out):
    for b in range(H * C):
        block = cot[b // C, b % C, 0:256, :]
        part = lax.dot_general(block, masked[...], (((0,), (0,)), ((), ())), preferred_element_type=F32).astype(BF)
        for c in range(BD):
            out[8 * b : 8 * b + 8, c] = part[:, c * P2 : (c + 1) * P2].reshape(8, DS, P2)


def sum_xy_body(parts, out):
    total = parts[0].astype(F32)
    for i in range(1, X * Y):
        total = total + parts[i].astype(F32)
    total = total.astype(BF)
    for h in range(H):
        out[:, h] = total


def sum_l_body(parts, out):
    total = parts[0].astype(F32)
    for i in range(1, L):
        total = total + parts[i].astype(F32)
    out[...] = total.astype(BF)


def hidden_grad_body(grads, weight, out):
    rows = HID * DS
    n = H * BD * DS
    prod = lax.dot_general(weight[...], grads[...], (((1,), (1,)), ((), ())), preferred_element_type=F32)
    keep = iota((rows, n), 0) % DS == iota((rows, n), 1) % DS
    prod = jnp.where(keep, prod, 0.0).reshape(HID, DS, n).sum(axis=1)
    pick = (iota((n // DS, n), 1) // DS == iota((n // DS, n), 0)).astype(F32)
    part = lax.dot_general(pick, prod, (((1,), (1,)), ((), ())), precision=HIGHEST, preferred_element_type=F32)
    for to in range(L * C):
        out[to] = part


def spread_body(parts, out):
    sums = []
    for c in range(C):
        total = parts[c]
        for l in range(1, L):
            total = total + parts[l * C + c]
        sums.append(total)
    total = jnp.concatenate(sums, axis=0)
    for to in range(X * Y):
        out[to] = total


def final_body(parts, slope, features, sensor_hot, first, sensor):
    total = parts[0]
    for i in range(1, X * Y):
        total = total + parts[i]
    grad_pre = total * slope[...]
    across = (((0,), (0,)), ((), ()))
    first[...] = lax.dot_general(features[...], grad_pre, across, precision=HIGHEST, preferred_element_type=F32)
    sensor[...] = lax.dot_general(sensor_hot[...], grad_pre, across, precision=HIGHEST, preferred_element_type=F32)


def out_grad_body(hidden_t, grads, out):
    n = H * C * BD * DS
    wide = (iota((n // DS, n), 1) // DS == iota((n // DS, n), 0)).astype(F32).astype(BF)
    spread = jnp.dot(hidden_t[...], wide, preferred_element_type=F32)
    keep = iota((DS, n), 0) == iota((DS, n), 1) % DS
    left = jnp.where(keep[None], spread[:, None, :], 0.0).reshape(HID * DS, n).astype(BF)
    out[...] = jnp.dot(left, grads[...], preferred_element_type=F32)


def gather(part, axes, count):
    return lax.all_to_all(jnp.broadcast_to(part[None], (count, *part.shape)), axes, 0, 0, tiled=True)


def local(
    pixels, cotangent, avail, band_index, band_sensor, wave_table, first_weight, sensor_embed, out_weight
):
    rows = pixels.shape[0]
    place = (lax.axis_index("x") * Y + lax.axis_index("y")) * L + lax.axis_index("l")
    tile = (place * rows) // TILE_PATCHES
    mask = lax.dynamic_slice_in_dim(avail, tile, 1, 0).astype(BF)
    masked = (pixels * mask[:, :, None]).reshape(rows, BD * P2)
    weight = out_weight.reshape(HID * DS, P2)

    (part,) = call(
        kernel_body, [((L, BD * DS, P2), BF)], [SMEM, SMEM, SMEM, VMEM, VMEM, VMEM],
        band_index, band_sensor, wave_table, first_weight, sensor_embed, weight, flops=2**25, vmem=60,
    )
    part_l = lax.all_to_all(part, "l", 0, 0, tiled=True)

    ids = jnp.concatenate([band_index, band_sensor]).astype(BF)
    tail = jnp.pad(ids[None], ((0, 15), (0, cotangent.shape[1] - 2 * BD)))
    cot_own = jnp.concatenate([cotangent, tail], axis=0)
    cot_own, part_l = lax.optimization_barrier((cot_own, part_l))
    kernels = gather(part_l.reshape(L * BD * DS, P2), ("x", "y"), X * Y).reshape(X * Y * L, BD, DS, P2)
    cot = lax.all_gather(cot_own, ("h", "c"), axis=0, tiled=False).reshape(H, C, rows + 16, 128)
    (grads,) = call(grad_body, [((X * Y * L, BD, DS, P2), BF)], [VMEM, VMEM], cot, masked, flops=2**28)

    grads, kernels = lax.optimization_barrier((grads, kernels))
    grads = lax.all_to_all(grads.reshape(X * Y, L, BD * DS, P2), ("x", "y"), 0, 0, tiled=True)
    shape = ((H, rows, 128), BF)
    keep, send = call(embed_body, [shape, shape], [VMEM, VMEM], masked, kernels, flops=2**28)
    other = lax.ppermute(send, "c", [(0, 1), (1, 0)])
    shares = call(pair_body, [((rows, 128), BF)] * H, [VMEM, VMEM], keep, other, flops=2**18)
    up, down = [(i, (i + 1) % H) for i in range(H)], [(i, (i - 1) % H) for i in range(H)]
    first = lax.ppermute(shares[2], "h", up)
    third = lax.ppermute(shares[3], "h", down)
    (second,) = call(add_body, [((rows, 128), BF)], [VMEM] * 2, shares[1], first, flops=2**16)
    second = lax.ppermute(second, "h", up)

    grads, *_ = lax.optimization_barrier((grads, first, third))
    (grads,) = call(sum_xy_body, [((L, H, BD * DS, P2), BF)], [VMEM], grads, flops=2**20)
    grads = lax.all_to_all(grads.reshape(L * H, BD * DS, P2), ("l", "h"), 0, 0, tiled=True)
    (grads,) = call(sum_l_body, [((H, BD * DS, P2), BF)], [VMEM], grads.reshape(L, H, BD * DS, P2), flops=2**18)
    mine = grads.reshape(H * BD * DS, P2)
    grads = lax.all_gather(mine, "c", axis=0, tiled=True)

    every = cot[:, :, rows, : 2 * BD].astype(jnp.int32).swapaxes(0, 1).reshape(C * H, 2 * BD)
    features, sensor_hot, preact = hypernet(
        every[:, :BD].reshape(-1), every[:, BD:].reshape(-1), wave_table, first_weight, sensor_embed
    )
    hidden_t = jax.nn.silu(preact).astype(BF).T
    slope = silu_slope(preact)

    (embed,) = call(join_body, [((rows, 128), BF)], [VMEM] * 3, shares[0], second, third, flops=2**18)
    bands = C * H * BD
    (parts,) = call(hidden_grad_body, [((L * C, bands // C, HID), F32)], [VMEM, VMEM], mine, weight, flops=2**28)
    parts = lax.all_to_all(parts, ("l", "c"), 0, 0, tiled=True)
    parts, *_ = lax.optimization_barrier((parts, second))
    (parts,) = call(spread_body, [((X * Y, bands, HID), F32)], [VMEM], parts, flops=2**16)
    parts = lax.all_to_all(parts, ("x", "y"), 0, 0, tiled=True)
    (grad_out,) = call(out_grad_body, [((HID * DS, P2), F32)], [VMEM, VMEM], hidden_t, grads, flops=2**28)
    grad_first, grad_sensor = call(
        final_body, [(first_weight.shape, F32), (sensor_embed.shape, F32)], [VMEM] * 4,
        parts, slope, features, sensor_hot, flops=2**20,
    )
    return (embed, grad_out.reshape(HID, DS, P2), grad_first, grad_sensor)


def solution(mesh):
    fine = Mesh(mesh.devices.reshape(X, Y, L, H, C), ("x", "y", "l", "h", "c"))
    patch, band = ("x", "y", "l"), ("h", "c")
    return jax.shard_map(
        local,
        mesh=fine,
        in_specs=(
            P(patch, band, None),
            P(patch, band),
            P(None, band),
            P(band),
            P(band),
            P(),
            P(),
            P(),
            P(None, patch, None),
        ),
        out_specs=(P(patch, band), P(None, patch, None), P(), P()),
        check_vma=False,
    )
```

```python
import functools
import math

import jax
import jax.numpy as jnp
from jax import lax
from jax.experimental import pallas as pl
from jax.experimental.pallas import tpu as pltpu
from jax.sharding import Mesh
from jax.sharding import PartitionSpec as P

TILE_PATCHES = 1024
X, Y, L, H, C = 4, 4, 4, 4, 2
BD = 2
DS = 16
P2 = 256
HID = 128
BF = jnp.bfloat16
F32 = jnp.float32
HIGHEST = lax.Precision.HIGHEST
VMEM = pl.BlockSpec(memory_space=pltpu.VMEM)
SMEM = pl.BlockSpec(memory_space=pltpu.SMEM)


def call(body, outs, specs, *args, flops=0, nbytes=2**20, vmem=24):
    return pl.pallas_call(
        body,
        out_shape=[jax.ShapeDtypeStruct(shape, dtype) for shape, dtype in outs],
        in_specs=specs,
        out_specs=[VMEM] * len(outs),
        compiler_params=pltpu.CompilerParams(vmem_limit_bytes=vmem * 2**20),
        cost_estimate=pl.CostEstimate(flops=flops, bytes_accessed=nbytes, transcendentals=0),
    )(*args)


def iota(shape, dim):
    return lax.broadcasted_iota(jnp.int32, shape, dim)


def wave_features(waves, width):
    half = width // 2
    steps = jnp.arange(half, dtype=F32)
    freqs = jnp.exp(steps * (math.log(100.0) / half))
    angles = waves[:, None] * freqs[None, :]
    return jnp.concatenate([jnp.sin(angles), jnp.cos(angles)], axis=1)


def silu_slope(preact):
    sigma = jax.nn.sigmoid(preact)
    return sigma * (1.0 + preact * (1.0 - sigma))


def hypernet(band_index, band_sensor, wave_table, first_weight, sensor_embed):
    table_hot = (
        band_index[:, None] == jnp.arange(wave_table.shape[0], dtype=jnp.int32)[None, :]
    ).astype(F32)
    waves = jnp.dot(table_hot, wave_table, precision=HIGHEST)
    features = wave_features(waves, first_weight.shape[0])
    sensor_hot = (
        band_sensor[:, None] == jnp.arange(sensor_embed.shape[0], dtype=jnp.int32)[None, :]
    ).astype(F32)
    preact = jnp.dot(features, first_weight, precision=HIGHEST) + jnp.dot(
        sensor_hot, sensor_embed, precision=HIGHEST
    )
    return (features, sensor_hot, preact)


def kernel_body(idx, sens, table, first, sensor, weight, out):
    lane = iota((8, HID), 1)
    half = HID // 2
    step = jnp.where(lane < half, lane, lane - half).astype(F32)
    freqs = jnp.exp(step * (math.log(100.0) / half))
    row = iota((8, HID), 0)
    waves = jnp.where(row == 0, table[idx[0]], table[idx[1]])
    angles = waves * freqs
    features = jnp.where(lane < half, jnp.sin(angles), jnp.cos(angles))
    preact = jnp.dot(features, first[...], precision=HIGHEST, preferred_element_type=F32)
    preact = preact + jnp.where(row == 0, sensor[pl.ds(sens[0], 1), :], sensor[pl.ds(sens[1], 1), :])
    hidden = (preact / (1.0 + jnp.exp(-preact))).astype(BF)
    wide = (iota((HID, HID * DS), 1) // DS == iota((HID, HID * DS), 0)).astype(F32).astype(BF)
    spread = jnp.dot(hidden, wide, preferred_element_type=F32)
    own = iota((DS, HID * DS), 1) % DS == iota((DS, HID * DS), 0)
    left = jnp.concatenate([jnp.where(own, spread[c : c + 1], 0.0) for c in range(BD)], axis=0).astype(BF)
    part = jnp.dot(left, weight[...], preferred_element_type=F32).astype(BF)
    for to in range(L):
        out[to] = part


def embed_body(masked, kernels, keep, send):
    core, high = lax.axis_index("c"), lax.axis_index("h")
    for step in range(H):
        to = lax.rem(high + step, H)
        for out, side in ((keep, core), (send, 1 - core)):
            first = 8 * (to * C + side)
            total = None
            for c in range(BD):
                right = kernels[pl.ds(first, 8), c].reshape(8 * DS, P2)
                term = lax.dot_general(
                    masked[:, c * P2 : (c + 1) * P2], right, (((1,), (1,)), ((), ())), preferred_element_type=F32
                )
                total = term if total is None else total + term
            out[step] = total.astype(BF)


def pair_body(keep, other, *outs):
    for step in range(H):
        outs[step][...] = (keep[step].astype(F32) + other[step].astype(F32)).astype(BF)


def add_body(a, b, out):
    out[...] = (a[...].astype(F32) + b[...].astype(F32)).astype(BF)


def join_body(a, b, c, out):
    out[...] = (a[...].astype(F32) + b[...].astype(F32) + c[...].astype(F32)).astype(BF)


def grad_body(cot, masked, out):
    for b in range(H * C):
        block = cot[b // C, b % C, 0:256, :]
        part = lax.dot_general(block, masked[...], (((0,), (0,)), ((), ())), preferred_element_type=F32).astype(BF)
        for c in range(BD):
            out[8 * b : 8 * b + 8, c] = part[:, c * P2 : (c + 1) * P2].reshape(8, DS, P2)


def sum_xy_body(parts, out):
    total = parts[0].astype(F32)
    for i in range(1, X * Y):
        total = total + parts[i].astype(F32)
    total = total.astype(BF)
    for h in range(H):
        out[:, h] = total


def sum_l_body(parts, out):
    total = parts[0].astype(F32)
    for i in range(1, L):
        total = total + parts[i].astype(F32)
    out[...] = total.astype(BF)


def hidden_grad_body(grads, weight, out):
    rows = HID * DS
    n = H * BD * DS
    prod = lax.dot_general(weight[...], grads[...], (((1,), (1,)), ((), ())), preferred_element_type=F32)
    keep = iota((rows, n), 0) % DS == iota((rows, n), 1) % DS
    prod = jnp.where(keep, prod, 0.0).reshape(HID, DS, n).sum(axis=1)
    pick = (iota((n // DS, n), 1) // DS == iota((n // DS, n), 0)).astype(F32)
    part = lax.dot_general(pick, prod, (((1,), (1,)), ((), ())), precision=HIGHEST, preferred_element_type=F32)
    for to in range(L * C):
        out[to] = part


def spread_body(parts, out):
    sums = []
    for c in range(C):
        total = parts[c]
        for l in range(1, L):
            total = total + parts[l * C + c]
        sums.append(total)
    total = jnp.concatenate(sums, axis=0)
    for to in range(X * Y):
        out[to] = total


def final_body(parts, slope, features, sensor_hot, first, sensor):
    total = parts[0]
    for i in range(1, X * Y):
        total = total + parts[i]
    grad_pre = total * slope[...]
    across = (((0,), (0,)), ((), ()))
    first[...] = lax.dot_general(features[...], grad_pre, across, precision=HIGHEST, preferred_element_type=F32)
    sensor[...] = lax.dot_general(sensor_hot[...], grad_pre, across, precision=HIGHEST, preferred_element_type=F32)


def out_grad_body(hidden_t, grads, out):
    n = H * C * BD * DS
    wide = (iota((n // DS, n), 1) // DS == iota((n // DS, n), 0)).astype(F32).astype(BF)
    spread = jnp.dot(hidden_t[...], wide, preferred_element_type=F32)
    keep = iota((DS, n), 0) == iota((DS, n), 1) % DS
    left = jnp.where(keep[None], spread[:, None, :], 0.0).reshape(HID * DS, n).astype(BF)
    out[...] = jnp.dot(left, grads[...], preferred_element_type=F32)


def gather(part, axes, count):
    return lax.all_to_all(jnp.broadcast_to(part[None], (count, *part.shape)), axes, 0, 0, tiled=True)


def local(
    pixels, cotangent, avail, band_index, band_sensor, wave_table, first_weight, sensor_embed, out_weight
):
    rows = pixels.shape[0]
    place = (lax.axis_index("x") * Y + lax.axis_index("y")) * L + lax.axis_index("l")
    tile = (place * rows) // TILE_PATCHES
    mask = lax.dynamic_slice_in_dim(avail, tile, 1, 0).astype(BF)
    masked = (pixels * mask[:, :, None]).reshape(rows, BD * P2)
    weight = out_weight.reshape(HID * DS, P2)

    (part,) = call(
        kernel_body, [((L, BD * DS, P2), BF)], [SMEM, SMEM, SMEM, VMEM, VMEM, VMEM],
        band_index, band_sensor, wave_table, first_weight, sensor_embed, weight, flops=2**25, vmem=60,
    )
    part_l = lax.all_to_all(part, "l", 0, 0, tiled=True)

    ids = jnp.concatenate([band_index, band_sensor]).astype(BF)
    tail = jnp.pad(ids[None], ((0, 15), (0, cotangent.shape[1] - 2 * BD)))
    cot_own = jnp.concatenate([cotangent, tail], axis=0)
    cot_own, part_l = lax.optimization_barrier((cot_own, part_l))
    kernels = gather(part_l.reshape(L * BD * DS, P2), ("x", "y"), X * Y).reshape(X * Y * L, BD, DS, P2)
    cot = lax.all_gather(cot_own, ("h", "c"), axis=0, tiled=False).reshape(H, C, rows + 16, 128)
    (grads,) = call(grad_body, [((X * Y * L, BD, DS, P2), BF)], [VMEM, VMEM], cot, masked, flops=2**28)

    grads, kernels = lax.optimization_barrier((grads, kernels))
    grads = lax.all_to_all(grads.reshape(X * Y, L, BD * DS, P2), ("x", "y"), 0, 0, tiled=True)
    shape = ((H, rows, 128), BF)
    keep, send = call(embed_body, [shape, shape], [VMEM, VMEM], masked, kernels, flops=2**28)
    other = lax.ppermute(send, "c", [(0, 1), (1, 0)])
    shares = call(pair_body, [((rows, 128), BF)] * H, [VMEM, VMEM], keep, other, flops=2**18)
    up, down = [(i, (i + 1) % H) for i in range(H)], [(i, (i - 1) % H) for i in range(H)]
    first = lax.ppermute(shares[2], "h", up)
    third = lax.ppermute(shares[3], "h", down)
    (second,) = call(add_body, [((rows, 128), BF)], [VMEM] * 2, shares[1], first, flops=2**16)
    second = lax.ppermute(second, "h", up)

    grads, *_ = lax.optimization_barrier((grads, first))
    (grads,) = call(sum_xy_body, [((L, H, BD * DS, P2), BF)], [VMEM], grads, flops=2**20)
    grads = lax.all_to_all(grads.reshape(L * H, BD * DS, P2), ("l", "h"), 0, 0, tiled=True)
    grads, *_ = lax.optimization_barrier((grads, third))
    (grads,) = call(sum_l_body, [((H, BD * DS, P2), BF)], [VMEM], grads.reshape(L, H, BD * DS, P2), flops=2**18)
    mine = grads.reshape(H * BD * DS, P2)
    grads = lax.all_gather(mine, "c", axis=0, tiled=True)

    every = cot[:, :, rows, : 2 * BD].astype(jnp.int32).swapaxes(0, 1).reshape(C * H, 2 * BD)
    features, sensor_hot, preact = hypernet(
        every[:, :BD].reshape(-1), every[:, BD:].reshape(-1), wave_table, first_weight, sensor_embed
    )
    hidden_t = jax.nn.silu(preact).astype(BF).T
    slope = silu_slope(preact)

    (embed,) = call(join_body, [((rows, 128), BF)], [VMEM] * 3, shares[0], second, third, flops=2**18)
    bands = C * H * BD
    (parts,) = call(hidden_grad_body, [((L * C, bands // C, HID), F32)], [VMEM, VMEM], mine, weight, flops=2**28)
    parts = lax.all_to_all(parts, ("l", "c"), 0, 0, tiled=True)
    (grad_out,) = call(out_grad_body, [((HID * DS, P2), F32)], [VMEM, VMEM], hidden_t, grads, flops=2**28)
    parts, *_ = lax.optimization_barrier((parts, second, grad_out))
    (parts,) = call(spread_body, [((X * Y, bands, HID), F32)], [VMEM], parts, flops=2**16)
    parts = lax.all_to_all(parts, ("x", "y"), 0, 0, tiled=True)
    grad_first, grad_sensor = call(
        final_body, [(first_weight.shape, F32), (sensor_embed.shape, F32)], [VMEM] * 4,
        parts, slope, features, sensor_hot, flops=2**20,
    )
    return (embed, grad_out.reshape(HID, DS, P2), grad_first, grad_sensor)


def solution(mesh):
    fine = Mesh(mesh.devices.reshape(X, Y, L, H, C), ("x", "y", "l", "h", "c"))
    patch, band = ("x", "y", "l"), ("h", "c")
    return jax.shard_map(
        local,
        mesh=fine,
        in_specs=(
            P(patch, band, None),
            P(patch, band),
            P(None, band),
            P(band),
            P(band),
            P(),
            P(),
            P(),
            P(None, patch, None),
        ),
        out_specs=(P(patch, band), P(None, patch, None), P(), P()),
        check_vma=False,
    )
```
